32 devices in a mesh: leaf: 32 (over z, y, x, core).
Axes of the slice: x: 2, y: 2, z: 4, core: 2. Of those that a mesh axis runs over, the one named last changes fastest.
Arguments:
- vectors: bfloat16 [64, 262144], P(None, 'leaf'), may hold values from -6 to 6
- leaf_basis: bfloat16 [64, 262144], P(None, 'leaf'), may hold values from -0.375 to 0.375
- local_transfer: bfloat16 [2016, 64, 64], P('leaf'), may hold values from -0.625 to 0.625
- near_tiles: bfloat16 [3072, 256, 256], P('leaf'), may hold values from -0.375 to 0.375
- near_rows: int32 [3072], P('leaf'), may hold values from 0 to 31, as said below
- near_cols: int32 [3072], P('leaf'), may hold values from 0 to 63, as said below
- far_tiles: bfloat16 [4608, 64, 64], P('leaf'), may hold values from -0.75 to 0.75
- far_rows: int32 [4608], P('leaf'), may hold values from 0 to 62, as said below
- far_cols: int32 [4608], P('leaf'), may hold values from 0 to 62, as said below
- far_counts: int32 [32, 9], P('leaf'), may hold values from 0 to 16, as said below
- top_transfer: float32 [30, 64, 64], replicated, may hold values from -0.625 to 0.625
- top_couple: float32 [31, 64, 64], replicated, may hold values from -0.75 to 0.75
Outputs:
- product: float32 [64, 262144], P(None, 'leaf')
The draws below stay inside these ranges and needn't reach their ends.
Inputs may be any that keep to these rules, and one draw needn't show every extreme that they name: `near_rows`: a leaf of the tile's own device, by its index there. `near_cols`: at least near_rows and at most near_rows + 32; a value v of 32 or more names leaf v - 32 of the next device, and never occurs on the last device. `far_rows`: a local node id on the owner; a slot's two nodes are on the same level, and differ on a device's slots with itself. `far_cols`: a local node id on the peer. `far_counts`: 0 exactly where the owner plus the offset passes the last device, else at least 1; column 0 is 16.
All inputs are finite; a program needn't handle non-finite values.
Results may differ from the reference program's by a relative error of at most 0.0075.
Values may be sent and summed in bfloat16 or wider, within the bound.
A program may use at most 192 MiB of HBM per device.

```python
import jax
import jax.numpy as jnp
from jax import lax

LEAF = 256
RANK = 64
VECS = 64
LEAVES_DEV = 32
NEAR_PER = 3
REACH = 8
CAP = 16
LEVELS = 5
TOPL = 5
NODES_DEV = 63
POINTS = 262144
NEAR = 3072
FAR = 4608
N_LEAF = 32


def far_pairs(key):
    slot_index = jnp.arange(FAR, dtype=jnp.int32)
    offset_of = slot_index // CAP % (REACH + 1)
    key_level, key_first, key_other, key_shift = jax.random.split(key, 4)
    height = jax.random.randint(key_level, (FAR,), 0, LEVELS + 1, dtype=jnp.int32)
    same_device = offset_of == 0
    height = jnp.where(same_device, height % LEVELS, height)
    level_size = jnp.right_shift(jnp.int32(LEAVES_DEV), height)
    offset = 2 * LEAVES_DEV - jnp.right_shift(jnp.int32(2 * LEAVES_DEV), height)
    first_pick = jax.random.randint(key_first, (FAR,), 0, 1 << 20, dtype=jnp.int32) % level_size
    other_pick = jax.random.randint(key_other, (FAR,), 0, 1 << 20, dtype=jnp.int32) % level_size
    move_pick = 1 + jax.random.randint(key_shift, (FAR,), 0, 1 << 20, dtype=jnp.int32) % jnp.maximum(level_size - 1, 1)
    second_pick = jnp.where(same_device, (first_pick + move_pick) % level_size, other_pick)
    rows_out = (offset + first_pick).astype(jnp.int32)
    cols_out = (offset + second_pick).astype(jnp.int32)
    rows_out = rows_out.at[0].set(0).at[CAP].set(NODES_DEV - 1).at[2 * CAP].set(0)
    cols_out = cols_out.at[0].set(1).at[CAP].set(NODES_DEV - 1).at[2 * CAP].set(0)
    return (rows_out, cols_out)


def near_pairs(key):
    per_device = NEAR_PER * LEAVES_DEV
    slot_index = jnp.arange(NEAR, dtype=jnp.int32)
    device = slot_index // per_device
    key_rows, key_reach, key_spot = jax.random.split(key, 3)
    rows_out = jax.random.randint(key_rows, (NEAR,), 0, LEAVES_DEV, dtype=jnp.int32)
    reach = jax.random.randint(key_reach, (NEAR,), 0, LEAVES_DEV + 1, dtype=jnp.int32)
    cols_out = rows_out + reach
    cols_out = jnp.where(device == N_LEAF - 1, jnp.minimum(cols_out, LEAVES_DEV - 1), cols_out)
    spot = jax.random.randint(key_spot, (), 0, per_device, dtype=jnp.int32)
    second_spot = (spot + 1) % per_device
    rows_out = rows_out.at[spot].set(LEAVES_DEV - 1).at[second_spot].set(0)
    cols_out = cols_out.at[spot].set(2 * LEAVES_DEV - 1).at[second_spot].set(0)
    return (rows_out.astype(jnp.int32), cols_out.astype(jnp.int32))


def draw_far_rows(key, part):
    shared = far_pairs(key)
    return shared[0]


def draw_far_cols(key, part):
    shared = far_pairs(key)
    return shared[1]


def draw_near_rows(key, part):
    shared = near_pairs(jax.random.fold_in(key, 5))
    return shared[0]


def draw_near_cols(key, part):
    shared = near_pairs(jax.random.fold_in(key, 5))
    return shared[1]


def draw_far_counts(key, part):
    key = jax.random.fold_in(key, 7)
    counts_out = jax.random.randint(key, (N_LEAF, REACH + 1), 1, CAP + 1, dtype=jnp.int32)
    owner = jnp.arange(N_LEAF, dtype=jnp.int32)[:, None]
    offset_of = jnp.arange(REACH + 1, dtype=jnp.int32)[None, :]
    counts_out = jnp.where(offset_of == 0, CAP, counts_out)
    counts_out = jnp.where(owner + offset_of >= N_LEAF, 0, counts_out)
    return counts_out.astype(jnp.int32)


def shard_levels(stream_key, dims, cuts, least, high):
    level = 1.0
    for axis_at, blocks in cuts:
        heights = jax.random.uniform(jax.random.fold_in(jax.random.fold_in(stream_key, 6), axis_at), (blocks,), jnp.float32, least / len(cuts), high / len(cuts))
        level = level * jnp.repeat(jnp.exp(heights), dims[axis_at] // blocks).reshape((-1,) + (1,) * (len(dims) - 1 - axis_at))
    return level


def bell_draw(rng, shape, spread, limit, cuts=(), kind=jnp.bfloat16):
    loudness = shard_levels(rng, shape, cuts, -0.22, 0.18) if cuts else 1.0
    entries = jax.random.normal(rng, shape, jnp.float32) * spread * loudness
    return jnp.minimum(jnp.maximum(entries, -limit), limit).astype(kind)


def setup_inputs(seed: int = 0) -> dict:
    key_list = jax.random.split(jax.random.key(seed), 13)
    return {
        "vectors": bell_draw(key_list[0], (VECS, POINTS), 1.0, 6.0, ((1, 32),)),
        "leaf_basis": bell_draw(key_list[1], (RANK, POINTS), LEAF ** -0.5, 0.375, ((1, 32),)),
        "local_transfer": bell_draw(key_list[2], (N_LEAF * NODES_DEV, RANK, RANK), (3 * RANK // 2) ** -0.5, 0.625, ((0, 32),)),
        "near_tiles": bell_draw(key_list[3], (NEAR, LEAF, LEAF), LEAF ** -0.5, 0.375, ((0, 32),)),
        "near_rows": draw_near_rows(jax.random.fold_in(key_list[12], 71), 0),
        "near_cols": draw_near_cols(jax.random.fold_in(key_list[12], 71), 0),
        "far_tiles": bell_draw(key_list[6], (FAR, RANK, RANK), RANK ** -0.5, 0.75, ((0, 32),)),
        "far_rows": draw_far_rows(jax.random.fold_in(key_list[12], 71), 0),
        "far_cols": draw_far_cols(jax.random.fold_in(key_list[12], 71), 0),
        "far_counts": draw_far_counts(jax.random.fold_in(key_list[12], 71), 0),
        "top_transfer": bell_draw(key_list[10], (N_LEAF - 2, RANK, RANK), (3 * RANK // 2) ** -0.5, 0.625, (), jnp.float32),
        "top_couple": bell_draw(key_list[11], (N_LEAF - 1, RANK, RANK), RANK ** -0.5, 0.75, (), jnp.float32),
    }


highest = lax.Precision.HIGHEST


def tree_upward(leaf_coefs, transfers):
    levels = [leaf_coefs]
    current = leaf_coefs
    offset = 0
    level_size = LEAVES_DEV
    while level_size > 1:
        lifted = jnp.einsum('dnvk,dnkr->dnvr', current.astype(jnp.float32), transfers[:, offset:offset + level_size].astype(jnp.float32))
        current = lifted.reshape(N_LEAF, level_size // 2, 2, VECS, RANK).sum(axis=2).astype(jnp.bfloat16)
        offset = offset + level_size
        level_size = level_size // 2
        levels.append(current)
    return jnp.concatenate(levels, axis=1)


def near_field(vectors, near_tiles, near_rows, near_cols):
    leaf_total = LEAVES_DEV * N_LEAF
    blocks = vectors.reshape(VECS, leaf_total, LEAF).astype(jnp.float32)
    per_device = NEAR_PER * LEAVES_DEV
    tile_sets = near_tiles.reshape(N_LEAF, per_device, LEAF, LEAF)
    base_leaf = (jnp.arange(N_LEAF, dtype=jnp.int32) * LEAVES_DEV)[:, None]
    rows_all = (near_rows.reshape(N_LEAF, per_device) + base_leaf).astype(jnp.int32)
    cols_all = (near_cols.reshape(N_LEAF, per_device) + base_leaf).astype(jnp.int32)

    def add_device(result, pieces):
        tile_set, row_ids, col_ids = pieces
        tile_float = tile_set.astype(jnp.float32)
        from_cols = jnp.einsum('vnq,npq->vnp', blocks[:, col_ids], tile_float)
        from_rows = jnp.einsum('vnp,npq->vnq', blocks[:, row_ids], tile_float)
        result = result.at[:, row_ids].add(from_cols).at[:, col_ids].add(from_rows)
        return result, None

    start_value = jnp.zeros((VECS, leaf_total, LEAF), jnp.float32)
    result, unused = lax.scan(add_device, start_value, (tile_sets, rows_all, cols_all))
    return result


def far_field(node_coefs, far_tiles, far_rows, far_cols, far_counts):
    per_device = (REACH + 1) * CAP
    slot_index = jnp.arange(per_device, dtype=jnp.int32)
    offset_of = slot_index // CAP
    column_of = slot_index % CAP
    tile_sets = far_tiles.reshape(N_LEAF, per_device, RANK, RANK)
    rows_local = far_rows.reshape(N_LEAF, per_device)
    cols_local = far_cols.reshape(N_LEAF, per_device)
    coef_float = node_coefs.astype(jnp.float32)

    def add_device(result, pieces):
        device, tile_set, row_ids, col_ids, counts_row = pieces
        slot_used = (column_of < counts_row[offset_of]).astype(jnp.float32)[:, None, None]
        peer_of = jnp.minimum(device + offset_of, N_LEAF - 1)
        row_global = (device * NODES_DEV + row_ids).astype(jnp.int32)
        col_global = (peer_of * NODES_DEV + col_ids).astype(jnp.int32)
        tile_float = tile_set.astype(jnp.float32) * slot_used
        to_rows = jnp.einsum('nvj,nkj->nvk', coef_float[col_global], tile_float)
        to_cols = jnp.einsum('nvk,nkj->nvj', coef_float[row_global], tile_float)
        result = result.at[row_global].add(to_rows).at[col_global].add(to_cols)
        return result, None

    start_value = jnp.zeros((N_LEAF * NODES_DEV, VECS, RANK), jnp.float32)
    devices = jnp.arange(N_LEAF, dtype=jnp.int32)
    result, unused = lax.scan(add_device, start_value, (devices, tile_sets, rows_local, cols_local, far_counts))
    return result


def top_tree(root_coefs, root_transfers, top_transfer, top_couple):
    coef_level = root_coefs
    lift_level = jnp.einsum('nvk,nkr->nvr', root_coefs, root_transfers, precision=highest)
    couplings = []
    for height in range(TOPL):
        node_total = N_LEAF >> height
        tile_set = top_couple[node_total // 2 - 1:node_total - 1]
        to_left = jnp.einsum('jvq,jkq->jvk', coef_level[1::2], tile_set, precision=highest)
        to_right = jnp.einsum('jvk,jkq->jvq', coef_level[0::2], tile_set, precision=highest)
        couplings.append(jnp.stack([to_left, to_right], axis=1).reshape(node_total, VECS, RANK))
        if height + 1 < TOPL:
            coef_level = lift_level.reshape(node_total // 2, 2, VECS, RANK).sum(axis=1)
            lift_level = jnp.einsum('nvk,nkr->nvr', coef_level, top_transfer[node_total // 2 - 2:node_total - 2], precision=highest)
    going_down = couplings[TOPL - 1]
    for height in range(TOPL - 2, -1, -1):
        node_total = N_LEAF >> height
        if height == 0:
            transfer = root_transfers
        else:
            transfer = top_transfer[node_total - 2:2 * node_total - 2]
        parents = jnp.repeat(going_down, 2, axis=0)
        going_down = couplings[height] + jnp.einsum('nvr,nkr->nvk', parents, transfer, precision=highest)
    return going_down


def reference(vectors, leaf_basis, local_transfer, near_tiles, near_rows, near_cols, far_tiles, far_rows, far_cols, far_counts, top_transfer, top_couple):
    leaf_total = LEAVES_DEV * N_LEAF
    blocks = vectors.reshape(VECS, leaf_total, LEAF)
    bases_grid = leaf_basis.reshape(RANK, leaf_total, LEAF)
    leaf_coefs = jnp.einsum('vnp,knp->nvk', blocks.astype(jnp.float32), bases_grid.astype(jnp.float32)).astype(jnp.bfloat16)
    transfers = local_transfer.reshape(N_LEAF, NODES_DEV, RANK, RANK)
    node_coefs = tree_upward(leaf_coefs.reshape(N_LEAF, LEAVES_DEV, VECS, RANK), transfers)
    far_terms = far_field(node_coefs.reshape(N_LEAF * NODES_DEV, VECS, RANK), far_tiles, far_rows, far_cols, far_counts)
    far_terms = far_terms.reshape(N_LEAF, NODES_DEV, VECS, RANK)
    root_transfers = transfers[:, NODES_DEV - 1].astype(jnp.float32)
    top_down = top_tree(node_coefs[:, NODES_DEV - 1].astype(jnp.float32), root_transfers, top_transfer, top_couple)
    current = (far_terms[:, NODES_DEV - 1] + top_down)[:, None]
    offset = NODES_DEV - 1
    level_size = 1
    while level_size < LEAVES_DEV:
        level_size = level_size * 2
        offset = offset - level_size
        parents = jnp.repeat(current, 2, axis=1)
        current = far_terms[:, offset:offset + level_size] + jnp.einsum('dnvr,dnkr->dnvk', parents, transfers[:, offset:offset + level_size].astype(jnp.float32), precision=highest)
    leaf_down = current.reshape(leaf_total, VECS, RANK).astype(jnp.bfloat16)
    far_part = jnp.einsum('nvk,knp->vnp', leaf_down.astype(jnp.float32), bases_grid.astype(jnp.float32))
    near_part = near_field(vectors, near_tiles, near_rows, near_cols)
    return (near_part + far_part).reshape(VECS, leaf_total * LEAF)
```

```python
import functools

import jax
import jax.numpy as jnp
from jax import lax
from jax.experimental import pallas as pl
from jax.experimental.pallas import tpu as pltpu
from jax.sharding import PartitionSpec as P

f32 = jnp.float32
bf16 = jnp.bfloat16
highest = lax.Precision.HIGHEST
NT = (((1,), (1,)), ((), ()))
VMEM = pl.BlockSpec(memory_space=pltpu.VMEM)
SMEM = pl.BlockSpec(memory_space=pltpu.SMEM)
LIMIT = 56 * 1024 * 1024


def dot(a, b):
    return jnp.dot(a, b, preferred_element_type=f32)


def dot_nt(a, b):
    return lax.dot_general(a, b, NT, preferred_element_type=f32)


def dot_split(a, b):
    high = a.astype(bf16)
    low = (a - high.astype(f32)).astype(bf16)
    rows = a.shape[0]
    both = dot_nt(jnp.concatenate([high, low], axis=0), b)
    return both[:rows] + both[rows:]


def upward_kernel(leaf_count, leaf_size, vec_ref, basis_ref, pairs_ref, coef_ref, root_ref):
    current = []
    for leaf in range(leaf_count):
        span = slice(leaf * leaf_size, (leaf + 1) * leaf_size)
        current.append(dot_nt(vec_ref[:, span], basis_ref[:, span]).astype(bf16))
    offset = 0
    while True:
        for spot, value in enumerate(current):
            coef_ref[offset + spot] = value
        if len(current) == 1:
            break
        parents = []
        for pair in range(len(current) // 2):
            joined = jnp.concatenate([current[2 * pair], current[2 * pair + 1]], axis=1)
            parents.append(dot(joined, pairs_ref[offset // 2 + pair]).astype(bf16))
        offset += len(current)
        current = parents
    root_ref[...] = current[0]


def pack_kernel(
    count, cap, offsets, rows_ref, counts_ref, ids_ref, coef_ref, tiles_ref, coef_out, term_out
):
    me = lax.axis_index("leaf")
    slots = cap * offsets
    for step in range(1, offsets):
        source = lax.rem(me - step + count, count)

        @pl.loop(0, cap // 2)
        def _(pair):
            values = []
            terms = []
            for half in range(2):
                spot = 2 * pair + half
                slot = step * cap + spot
                values.append(coef_ref[ids_ref[source * slots + slot]])
                term = dot(coef_ref[rows_ref[slot]], tiles_ref[slot])
                used = spot < counts_ref[step]
                terms.append(jnp.where(used, term, 0.0).astype(bf16))
            coef_out[step - 1, pair] = jnp.concatenate(values, axis=1)
            term_out[step - 1, pair] = jnp.concatenate(terms, axis=1)


def exchange_kernel(
    count, reach, coef_in, term_in, coef_out, term_out, coef_send, coef_recv, term_send, term_recv
):
    me = lax.axis_index("leaf")
    barrier = pltpu.get_barrier_semaphore()
    for step in range(1, reach + 1):
        for sign in (-1, 1):
            peer = me + sign * step

            @pl.when((peer >= 0) & (peer < count))
            def _(peer=peer):
                pl.semaphore_signal(
                    barrier, inc=1, device_id=(peer,), device_id_type=pl.DeviceIdType.MESH
                )

    pl.semaphore_wait(barrier, jnp.minimum(me, reach) + jnp.minimum(count - 1 - me, reach))

    def back(step):
        return pltpu.make_async_remote_copy(
            src_ref=coef_in.at[step - 1],
            dst_ref=coef_out.at[step - 1],
            send_sem=coef_send.at[step - 1],
            recv_sem=coef_recv.at[step - 1],
            device_id=(me - step,),
            device_id_type=pl.DeviceIdType.MESH,
        )

    def ahead(step):
        return pltpu.make_async_remote_copy(
            src_ref=term_in.at[step - 1],
            dst_ref=term_out.at[step - 1],
            send_sem=term_send.at[step - 1],
            recv_sem=term_recv.at[step - 1],
            device_id=(me + step,),
            device_id_type=pl.DeviceIdType.MESH,
        )

    for step in range(reach, 0, -1):

        @pl.when(me - step >= 0)
        def _(step=step):
            back(step).start()

        @pl.when(me + step < count)
        def _(step=step):
            ahead(step).start()

    for step in range(1, reach + 1):

        @pl.when(me - step >= 0)
        def _(step=step):
            back(step).wait_send()
            ahead(step).wait_recv()

        @pl.when(me + step < count)
        def _(step=step):
            ahead(step).wait_send()
            back(step).wait_recv()


def near_kernel(
    group, steps, leaf_size, points, rows_ref, cols_ref, vec_ref, next_ref, tiles_ref, own_ref, spread_ref, joined, total
):
    step = pl.program_id(0)

    @pl.when(step == 0)
    def _():
        joined[:, :points] = vec_ref[...]
        joined[:, points:] = next_ref[...]
        total[...] = jnp.zeros_like(total)

    for spot in range(group):
        tile = tiles_ref[spot]
        row = pl.ds(pl.multiple_of(rows_ref[step * group + spot] * leaf_size, leaf_size), leaf_size)
        col = pl.ds(pl.multiple_of(cols_ref[step * group + spot] * leaf_size, leaf_size), leaf_size)
        to_row = dot_nt(joined[:, col], tile)
        to_col = dot(joined[:, row], tile)
        total[:, row] += to_row
        total[:, col] += to_col

    @pl.when(step == steps - 1)
    def _():
        own_ref[...] = total[:, :points]
        spread_ref[...] = total[:, points:].astype(bf16)


def downward_kernel(
    count,
    cap,
    offsets,
    leaf_count,
    leaf_size,
    rows_ref,
    cols_ref,
    counts_ref,
    ids_ref,
    coef_ref,
    tiles_ref,
    coef_got,
    term_got,
    roots_ref,
    transfer_ref,
    top_ref,
    couple_ref,
    pairs_ref,
    basis_ref,
    own_ref,
    got_ref,
    out_ref,
    far,
    level,
):
    me = lax.axis_index("leaf")
    slots = cap * offsets
    rank = coef_ref.shape[1]
    far[...] = jnp.zeros_like(far)

    @pl.loop(0, cap)
    def _(spot):
        tile = tiles_ref[spot]
        row = rows_ref[spot]
        col = cols_ref[spot]
        to_row = dot_nt(coef_ref[col], tile)
        to_col = dot(coef_ref[row], tile)

        @pl.when(spot < counts_ref[0])
        def _():
            far[row] += to_row
            far[col] += to_col

    for step in range(1, offsets):

        @pl.when(me + step < count)
        def _(step=step):
            @pl.loop(0, cap // 2)
            def _(pair):
                values = coef_got[step - 1, pair]
                for half in range(2):
                    spot = 2 * pair + half
                    slot = step * cap + spot
                    term = dot_nt(values[:, half * rank : (half + 1) * rank], tiles_ref[slot])
                    far[rows_ref[slot]] += jnp.where(spot < counts_ref[step], term, 0.0)

        @pl.when(me - step >= 0)
        def _(step=step):
            @pl.loop(0, cap // 2)
            def _(pair):
                values = term_got[step - 1, pair].astype(f32)
                for half in range(2):
                    slot = step * cap + 2 * pair + half
                    node = ids_ref[(me - step) * slots + slot]
                    far[node] += values[:, half * rank : (half + 1) * rank]

    for node in range(count // 2):
        left = roots_ref[2 * node]
        right = roots_ref[2 * node + 1]
        joined = jnp.concatenate([left[:, :rank], right[:, :rank]], axis=1)
        lift = jnp.concatenate([left[:, rank:], right[:, rank:]], axis=0)
        level[count // 2 + node] = dot(joined, lift)
        level[count + 2 * node] = left[:, :rank].astype(f32)
        level[count + 2 * node + 1] = right[:, :rank].astype(f32)
    for node in range(count // 2 - 1, 1, -1):
        joined = jnp.concatenate([level[2 * node], level[2 * node + 1]], axis=1)
        level[node] = jnp.dot(joined, top_ref[node - 1], precision=highest, preferred_element_type=f32)
    heights = count.bit_length() - 1
    heap = count + me
    going = None
    for height in range(heights - 1, -1, -1):
        node = heap >> height
        other = level[node ^ 1]
        tile = couple_ref[(node >> 1) - 1]
        turned = jnp.where(node % 2 == 0, tile.T, tile)
        term = jnp.dot(other, turned, precision=highest, preferred_element_type=f32)
        if going is None:
            going = term
        elif height == 0:
            going = term + dot_split(going, transfer_ref[...])
        else:
            lift = transfer_of(top_ref, node - 2, rank)
            going = term + lax.dot_general(going, lift, NT, precision=highest, preferred_element_type=f32)

    offset = far.shape[0] - 1
    current = [far[offset] + going]
    while len(current) < leaf_count:
        offset -= 2 * len(current)
        children = []
        for spot, value in enumerate(current):
            both = dot_split(value, pairs_ref[offset // 2 + spot])
            children.append(far[offset + 2 * spot] + both[:, :rank])
            children.append(far[offset + 2 * spot + 1] + both[:, rank:])
        current = children
    for leaf, value in enumerate(current):
        span = slice(leaf * leaf_size, (leaf + 1) * leaf_size)
        term = dot(value.astype(bf16), basis_ref[:, span])
        out_ref[:, span] = own_ref[:, span] + got_ref[:, span].astype(f32) + term


def transfer_of(top_ref, index, rank):
    start = pl.multiple_of((index % 2) * rank, rank)
    return top_ref[index // 2, pl.ds(start, rank), :]


def body(
    vectors,
    leaf_basis,
    local_transfer,
    near_tiles,
    near_rows,
    near_cols,
    far_tiles,
    far_rows,
    far_cols,
    far_counts,
    top_transfer,
    top_couple,
):
    vec_count, points = vectors.shape
    rank = leaf_basis.shape[0]
    near_count, leaf_size, _ = near_tiles.shape
    leaf_count = points // leaf_size
    nodes = local_transfer.shape[0]
    count = lax.axis_size("leaf")
    slots = far_tiles.shape[0]
    offsets = far_counts.shape[1]
    reach = offsets - 1
    cap = slots // offsets
    counts = far_counts[0]
    params = pltpu.CompilerParams(vmem_limit_bytes=LIMIT)

    following = lax.ppermute(vectors, "leaf", [(source, source - 1) for source in range(1, count)])
    ids = lax.all_gather(far_cols, "leaf", tiled=True)
    pairs = local_transfer[: nodes - 1].reshape(nodes // 2, 2 * rank, rank)
    root_transfer = local_transfer[nodes - 1]

    coefs, root = pl.pallas_call(
        functools.partial(upward_kernel, leaf_count, leaf_size),
        out_shape=[
            jax.ShapeDtypeStruct((nodes, vec_count, rank), bf16),
            jax.ShapeDtypeStruct((vec_count, rank), bf16),
        ],
        in_specs=[VMEM] * 3,
        out_specs=[VMEM] * 2,
        compiler_params=params,
        name="upward",
    )(vectors, leaf_basis, pairs)
    roots = lax.all_gather(jnp.concatenate([root, root_transfer], axis=1), "leaf")

    packed = jax.ShapeDtypeStruct((reach, cap // 2, vec_count, 2 * rank), bf16)
    coef_send, term_send = pl.pallas_call(
        functools.partial(pack_kernel, count, cap, offsets),
        out_shape=[packed, packed],
        in_specs=[SMEM] * 3 + [VMEM] * 2,
        out_specs=[VMEM] * 2,
        compiler_params=params,
        name="pack",
    )(far_rows, counts, ids, coefs, far_tiles)

    group = 8
    steps = near_count // group
    near_own, spread = pl.pallas_call(
        functools.partial(near_kernel, group, steps, leaf_size, points),
        out_shape=[
            jax.ShapeDtypeStruct((vec_count, points), f32),
            jax.ShapeDtypeStruct((vec_count, points), bf16),
        ],
        grid_spec=pltpu.PrefetchScalarGridSpec(
            num_scalar_prefetch=2,
            grid=(steps,),
            in_specs=[
                pl.BlockSpec((vec_count, points), lambda i, *_: (0, 0)),
                pl.BlockSpec((vec_count, points), lambda i, *_: (0, 0)),
                pl.BlockSpec((group, leaf_size, leaf_size), lambda i, *_: (i, 0, 0)),
            ],
            out_specs=[
                pl.BlockSpec((vec_count, points), lambda i, *_: (0, 0)),
                pl.BlockSpec((vec_count, points), lambda i, *_: (0, 0)),
            ],
            scratch_shapes=[
                pltpu.VMEM((vec_count, 2 * points), bf16),
                pltpu.VMEM((vec_count, 2 * points), f32),
            ],
        ),
        compiler_params=params,
        name="near",
    )(near_rows, near_cols, vectors, following, near_tiles)
    spread, coef_send, term_send = lax.optimization_barrier((spread, coef_send, term_send))
    near_got = lax.ppermute(spread, "leaf", [(source, source + 1) for source in range(count - 1)])

    any_space = pl.BlockSpec(memory_space=pl.ANY)
    coef_got, term_got = pl.pallas_call(
        functools.partial(exchange_kernel, count, reach),
        out_shape=[packed, packed],
        in_specs=[any_space] * 2,
        out_specs=[any_space] * 2,
        scratch_shapes=[pltpu.SemaphoreType.DMA((reach,))] * 4,
        compiler_params=pltpu.CompilerParams(collective_id=0, has_side_effects=True),
        name="exchange",
    )(coef_send, term_send)

    return pl.pallas_call(
        functools.partial(downward_kernel, count, cap, offsets, leaf_count, leaf_size),
        out_shape=jax.ShapeDtypeStruct((vec_count, points), f32),
        in_specs=[SMEM] * 4 + [VMEM] * 12,
        out_specs=VMEM,
        scratch_shapes=[
            pltpu.VMEM((nodes, vec_count, rank), f32),
            pltpu.VMEM((2 * count, vec_count, rank), f32),
        ],
        compiler_params=params,
        name="downward",
    )(
        far_rows,
        far_cols,
        counts,
        ids,
        coefs,
        far_tiles,
        coef_got,
        term_got,
        roots,
        root_transfer,
        top_transfer.reshape(count // 2 - 1, 2 * rank, rank),
        top_couple,
        pairs,
        leaf_basis,
        near_own,
        near_got,
    )


def solution(mesh):
    in_specs = (
        P(None, "leaf"),
        P(None, "leaf"),
        P("leaf", None, None),
        P("leaf", None, None),
        P("leaf"),
        P("leaf"),
        P("leaf", None, None),
        P("leaf"),
        P("leaf"),
        P("leaf", None),
        P(),
        P(),
    )
    out_specs = P(None, "leaf")
    return jax.shard_map(body, mesh=mesh, in_specs=in_specs, out_specs=out_specs, check_vma=False)
```

```python
import functools

import jax
import jax.numpy as jnp
from jax import lax
from jax.experimental import pallas as pl
from jax.experimental.pallas import tpu as pltpu
from jax.sharding import PartitionSpec as P

f32 = jnp.float32
bf16 = jnp.bfloat16
highest = lax.Precision.HIGHEST
NT = (((1,), (1,)), ((), ()))
VMEM = pl.BlockSpec(memory_space=pltpu.VMEM)
SMEM = pl.BlockSpec(memory_space=pltpu.SMEM)
LIMIT = 56 * 1024 * 1024


def dot(a, b):
    return jnp.dot(a, b, preferred_element_type=f32)


def dot_nt(a, b):
    return lax.dot_general(a, b, NT, preferred_element_type=f32)


def dot_split(a, b):
    high = a.astype(bf16)
    low = (a - high.astype(f32)).astype(bf16)
    rows = a.shape[0]
    both = dot_nt(jnp.concatenate([high, low], axis=0), b)
    return both[:rows] + both[rows:]


def pack_rows(value):
    half = value.shape[0] // 2
    return jnp.concatenate([value[:half], value[half:]], axis=1)


def unpack_rows(value):
    half = value.shape[1] // 2
    return jnp.concatenate([value[:, :half], value[:, half:]], axis=0)


def child_pair(transfer_ref, node):
    rank = transfer_ref.shape[1]
    return transfer_ref[node : node + 2].reshape(2 * rank, rank)


def greet_all(me, count):
    barrier = pltpu.get_barrier_semaphore()

    @pl.loop(1, count)
    def _(turn):
        pl.semaphore_signal(
            barrier, inc=1, device_id=(lax.rem(me + turn, count),), device_id_type=pl.DeviceIdType.MESH
        )

    pl.semaphore_wait(barrier, count - 1)


def remote(source, target, send, recv, peer):
    return pltpu.make_async_remote_copy(
        src_ref=source,
        dst_ref=target,
        send_sem=send,
        recv_sem=recv,
        device_id=(peer,),
        device_id_type=pl.DeviceIdType.MESH,
    )


def upward_kernel(
    count,
    leaf_count,
    leaf_size,
    reach,
    vec_ref,
    basis_ref,
    transfer_ref,
    cols_ref,
    coef_ref,
    root_ref,
    ids_ref,
    lifts_ref,
    lift_buf,
    id_send,
    id_recv,
    lift_send,
    lift_recv,
    own_sem,
):
    me = lax.axis_index("leaf")
    nodes = transfer_ref.shape[0]
    lift_buf[...] = pack_rows(transfer_ref[nodes - 1])
    greet_all(me, count)

    def id_copy(step):
        return remote(
            cols_ref, ids_ref.at[step - 1], id_send.at[step - 1], id_recv.at[step - 1], me + step
        )

    def lift_copy(turn):
        peer = lax.rem(me + turn, count)
        return remote(lift_buf, lifts_ref.at[me], lift_send.at[turn], lift_recv.at[turn], peer)

    for step in range(1, reach + 1):

        @pl.when(me + step < count)
        def _(step=step):
            id_copy(step).start()

    own = pltpu.make_async_copy(lift_buf, lifts_ref.at[me], own_sem)
    own.start()

    @pl.loop(1, count)
    def _(turn):
        lift_copy(turn).start()

    current = []
    for leaf in range(leaf_count):
        span = slice(leaf * leaf_size, (leaf + 1) * leaf_size)
        current.append(dot_nt(vec_ref[:, span], basis_ref[:, span]).astype(bf16))
    offset = 0
    while True:
        for spot, value in enumerate(current):
            coef_ref[offset + spot] = value
        if len(current) == 1:
            break
        parents = []
        for pair in range(len(current) // 2):
            joined = jnp.concatenate([current[2 * pair], current[2 * pair + 1]], axis=1)
            parents.append(dot(joined, child_pair(transfer_ref, offset + 2 * pair)).astype(bf16))
        offset += len(current)
        current = parents
    root_ref[...] = pack_rows(current[0])
    own.wait()

    @pl.loop(1, count)
    def _(turn):
        lift_copy(turn).wait()

    for step in range(1, reach + 1):

        @pl.when(me + step < count)
        def _(step=step):
            id_copy(step).wait_send()

        @pl.when(me - step >= 0)
        def _(step=step):
            id_copy(step).wait_recv()


def exchange_kernel(
    count,
    cap,
    offsets,
    rows_ref,
    counts_ref,
    ids_ref,
    coef_ref,
    tiles_ref,
    root_ref,
    coef_got,
    term_got,
    roots_ref,
    coef_buf,
    term_buf,
    coef_send,
    coef_recv,
    term_send,
    term_recv,
    root_send,
    root_recv,
    own_sem,
):
    me = lax.axis_index("leaf")
    reach = offsets - 1
    greet_all(me, count)

    def root_copy(turn):
        peer = lax.rem(me + turn, count)
        return remote(root_ref, roots_ref.at[me], root_send.at[turn], root_recv.at[turn], peer)

    def back(step):
        at = step - 1
        return remote(coef_buf.at[at], coef_got.at[at], coef_send.at[at], coef_recv.at[at], me - step)

    def ahead(step):
        at = step - 1
        return remote(term_buf.at[at], term_got.at[at], term_send.at[at], term_recv.at[at], me + step)

    own = pltpu.make_async_copy(root_ref, roots_ref.at[me], own_sem)
    own.start()

    for step in range(reach, 0, -1):

        @pl.when(me - step >= 0)
        def _(step=step):
            for pair in range(cap // 2):
                slot = step * cap + 2 * pair
                values = [coef_ref[ids_ref[step - 1, 0, slot + half]] for half in range(2)]
                coef_buf[step - 1, pair] = jnp.concatenate(values, axis=1)
            back(step).start()

        @pl.when(me + step < count)
        def _(step=step):
            for pair in range(cap // 2):
                terms = []
                for half in range(2):
                    spot = 2 * pair + half
                    slot = step * cap + spot
                    term = dot(coef_ref[rows_ref[slot]], tiles_ref[slot])
                    terms.append(jnp.where(spot < counts_ref[step], term, 0.0).astype(bf16))
                term_buf[step - 1, pair] = jnp.concatenate(terms, axis=1)
            ahead(step).start()

    @pl.loop(1, count)
    def _(turn):
        root_copy(turn).start()

    own.wait()

    @pl.loop(1, count)
    def _(turn):
        root_copy(turn).wait()

    for step in range(1, reach + 1):

        @pl.when(me - step >= 0)
        def _(step=step):
            back(step).wait_send()
            ahead(step).wait_recv()

        @pl.when(me + step < count)
        def _(step=step):
            ahead(step).wait_send()
            back(step).wait_recv()


def near_kernel(
    group, steps, leaf_size, points, rows_ref, cols_ref, vec_ref, next_ref, tiles_ref, own_ref, spread_ref, joined, total
):
    step = pl.program_id(0)

    @pl.when(step == 0)
    def _():
        joined[:, :points] = vec_ref[...]
        joined[:, points:] = next_ref[...]
        total[...] = jnp.zeros_like(total)

    for spot in range(group):
        tile = tiles_ref[spot]
        row = pl.ds(pl.multiple_of(rows_ref[step * group + spot] * leaf_size, leaf_size), leaf_size)
        col = pl.ds(pl.multiple_of(cols_ref[step * group + spot] * leaf_size, leaf_size), leaf_size)
        to_row = dot_nt(joined[:, col], tile)
        to_col = dot(joined[:, row], tile)
        total[:, row] += to_row
        total[:, col] += to_col

    @pl.when(step == steps - 1)
    def _():
        own_ref[...] = total[:, :points]
        spread_ref[...] = total[:, points:].astype(bf16)


def downward_kernel(
    count,
    cap,
    offsets,
    leaf_count,
    leaf_size,
    chunks,
    rows_ref,
    cols_ref,
    counts_ref,
    ids_ref,
    coef_ref,
    tiles_ref,
    coef_got,
    term_got,
    roots_ref,
    lifts_ref,
    transfer_ref,
    top_hbm,
    couple_hbm,
    basis_hbm,
    own_hbm,
    got_hbm,
    out_hbm,
    far,
    level,
    top_ref,
    couple_ref,
    basis_ref,
    own_ref,
    got_ref,
    load_sem,
    out_sem,
):
    me = lax.axis_index("leaf")
    rank = coef_ref.shape[1]
    late = [(top_hbm, top_ref), (couple_hbm, couple_ref), (basis_hbm, basis_ref)]
    late += [(own_hbm, own_ref), (got_hbm, got_ref)]
    loads = [pltpu.make_async_copy(a, b, load_sem.at[i]) for i, (a, b) in enumerate(late)]
    for load in loads:
        load.start()
    far[...] = jnp.zeros_like(far)

    to_row = []
    to_col = []
    for spot in range(cap):
        tile = tiles_ref[spot]
        used = spot < counts_ref[0]
        to_row.append(jnp.where(used, dot_nt(coef_ref[cols_ref[spot]], tile), 0.0))
        to_col.append(jnp.where(used, dot(coef_ref[rows_ref[spot]], tile), 0.0))
    for spot in range(cap):
        far[rows_ref[spot]] += to_row[spot]
        far[cols_ref[spot]] += to_col[spot]

    for step in range(1, offsets):

        @pl.when(me + step < count)
        def _(step=step):
            terms = []
            for spot in range(cap):
                half = spot % 2
                values = coef_got[step - 1, spot // 2][:, half * rank : (half + 1) * rank]
                term = dot_nt(values, tiles_ref[step * cap + spot])
                terms.append(jnp.where(spot < counts_ref[step], term, 0.0))
            for spot in range(cap):
                far[rows_ref[step * cap + spot]] += terms[spot]

        @pl.when(me - step >= 0)
        def _(step=step):
            for spot in range(cap):
                half = spot % 2
                values = term_got[step - 1, spot // 2][:, half * rank : (half + 1) * rank]
                far[ids_ref[step - 1, 0, step * cap + spot]] += values.astype(f32)

    loads[0].wait()
    loads[1].wait()
    for node in range(count // 2):
        left = unpack_rows(roots_ref[2 * node])
        right = unpack_rows(roots_ref[2 * node + 1])
        joined = jnp.concatenate([left, right], axis=1)
        lift = [unpack_rows(lifts_ref[2 * node + half]) for half in range(2)]
        level[count // 2 + node] = dot(joined, jnp.concatenate(lift, axis=0))
        level[count + 2 * node] = left.astype(f32)
        level[count + 2 * node + 1] = right.astype(f32)
    for node in range(count // 2 - 1, 1, -1):
        joined = jnp.concatenate([level[2 * node], level[2 * node + 1]], axis=1)
        level[node] = jnp.dot(joined, top_ref[node - 1], precision=highest, preferred_element_type=f32)
    heights = count.bit_length() - 1
    heap = count + me
    going = None
    for height in range(heights - 1, -1, -1):
        node = heap >> height
        other = level[node ^ 1]
        tile = couple_ref[(node >> 1) - 1]
        turned = jnp.where(node % 2 == 0, tile.T, tile)
        term = jnp.dot(other, turned, precision=highest, preferred_element_type=f32)
        if going is None:
            going = term
        elif height == 0:
            going = term + dot_split(going, transfer_ref[transfer_ref.shape[0] - 1])
        else:
            lift = transfer_of(top_ref, node - 2, rank)
            going = term + lax.dot_general(going, lift, NT, precision=highest, preferred_element_type=f32)

    offset = far.shape[0] - 1
    current = [far[offset] + going]
    while len(current) < leaf_count:
        offset -= 2 * len(current)
        children = []
        for spot, value in enumerate(current):
            both = dot_split(value, child_pair(transfer_ref, offset + 2 * spot))
            children.append(far[offset + 2 * spot] + both[:, :rank])
            children.append(far[offset + 2 * spot + 1] + both[:, rank:])
        current = children
    for load in loads[2:]:
        load.wait()
    width = leaf_count * leaf_size // chunks
    stores = []
    for leaf, value in enumerate(current):
        span = slice(leaf * leaf_size, (leaf + 1) * leaf_size)
        term = dot(value.astype(bf16), basis_ref[:, span])
        own_ref[:, span] = own_ref[:, span] + got_ref[:, span].astype(f32) + term
        if (leaf + 1) * leaf_size % width == 0:
            part = pl.ds(len(stores) * width, width)
            store = pltpu.make_async_copy(own_ref.at[:, part], out_hbm.at[:, part], out_sem.at[len(stores)])
            store.start()
            stores.append(store)
    for store in stores:
        store.wait()


def transfer_of(top_ref, index, rank):
    start = pl.multiple_of((index % 2) * rank, rank)
    return top_ref[index // 2, pl.ds(start, rank), :]


def body(
    vectors,
    leaf_basis,
    local_transfer,
    near_tiles,
    near_rows,
    near_cols,
    far_tiles,
    far_rows,
    far_cols,
    far_counts,
    top_transfer,
    top_couple,
):
    vec_count, points = vectors.shape
    rank = leaf_basis.shape[0]
    near_count, leaf_size, _ = near_tiles.shape
    leaf_count = points // leaf_size
    nodes = local_transfer.shape[0]
    count = lax.axis_size("leaf")
    slots = far_tiles.shape[0]
    offsets = far_counts.shape[1]
    reach = offsets - 1
    cap = slots // offsets
    counts = far_counts[0]
    params = pltpu.CompilerParams(vmem_limit_bytes=LIMIT)

    following = lax.ppermute(vectors, "leaf", [(source, source - 1) for source in range(1, count)])
    any_space = pl.BlockSpec(memory_space=pl.ANY)
    dma = pltpu.SemaphoreType.DMA
    half_rows = jax.ShapeDtypeStruct((count, rank // 2, 2 * rank), bf16)

    coefs, root, ids, lifts = pl.pallas_call(
        functools.partial(upward_kernel, count, leaf_count, leaf_size, reach),
        out_shape=[
            jax.ShapeDtypeStruct((nodes, vec_count, rank), bf16),
            jax.ShapeDtypeStruct((vec_count // 2, 2 * rank), bf16),
            jax.ShapeDtypeStruct((reach, 1, slots), jnp.int32),
            half_rows,
        ],
        in_specs=[VMEM] * 3 + [any_space],
        out_specs=[VMEM] * 2 + [any_space] * 2,
        scratch_shapes=[pltpu.VMEM((rank // 2, 2 * rank), bf16)]
        + [dma((reach,))] * 2
        + [dma((count,))] * 2
        + [dma(())],
        compiler_params=pltpu.CompilerParams(
            collective_id=0, has_side_effects=True, vmem_limit_bytes=LIMIT
        ),
        name="upward",
    )(vectors, leaf_basis, local_transfer, far_cols.reshape(1, slots))

    group = 8
    steps = near_count // group
    near_own, spread = pl.pallas_call(
        functools.partial(near_kernel, group, steps, leaf_size, points),
        out_shape=[
            jax.ShapeDtypeStruct((vec_count, points), f32),
            jax.ShapeDtypeStruct((vec_count, points), bf16),
        ],
        grid_spec=pltpu.PrefetchScalarGridSpec(
            num_scalar_prefetch=2,
            grid=(steps,),
            in_specs=[
                pl.BlockSpec((vec_count, points), lambda i, *_: (0, 0)),
                pl.BlockSpec((vec_count, points), lambda i, *_: (0, 0)),
                pl.BlockSpec((group, leaf_size, leaf_size), lambda i, *_: (i, 0, 0)),
            ],
            out_specs=[
                pl.BlockSpec((vec_count, points), lambda i, *_: (0, 0)),
                pl.BlockSpec((vec_count, points), lambda i, *_: (0, 0)),
            ],
            scratch_shapes=[
                pltpu.VMEM((vec_count, 2 * points), bf16),
                pltpu.VMEM((vec_count, 2 * points), f32),
            ],
        ),
        compiler_params=params,
        name="near",
    )(near_rows, near_cols, vectors, following, near_tiles)
    spread, coefs = lax.optimization_barrier((spread, coefs))
    near_got = lax.ppermute(spread, "leaf", [(source, source + 1) for source in range(count - 1)])

    packed = (reach, cap // 2, vec_count, 2 * rank)
    coef_got, term_got, roots = pl.pallas_call(
        functools.partial(exchange_kernel, count, cap, offsets),
        out_shape=[
            jax.ShapeDtypeStruct(packed, bf16),
            jax.ShapeDtypeStruct(packed, bf16),
            jax.ShapeDtypeStruct((count, vec_count // 2, 2 * rank), bf16),
        ],
        in_specs=[SMEM] * 3 + [VMEM] * 3,
        out_specs=[any_space] * 3,
        scratch_shapes=[pltpu.VMEM(packed, bf16)] * 2
        + [dma((reach,))] * 4
        + [dma((count,))] * 2
        + [dma(())],
        compiler_params=pltpu.CompilerParams(
            collective_id=1, has_side_effects=True, vmem_limit_bytes=LIMIT
        ),
        name="exchange",
    )(far_rows, counts, ids, coefs, far_tiles, root)

    chunks = 4
    top_pairs = top_transfer.reshape(count // 2 - 1, 2 * rank, rank)
    return pl.pallas_call(
        functools.partial(downward_kernel, count, cap, offsets, leaf_count, leaf_size, chunks),
        out_shape=jax.ShapeDtypeStruct((vec_count, points), f32),
        in_specs=[SMEM] * 4 + [VMEM] * 7 + [any_space] * 5,
        out_specs=any_space,
        scratch_shapes=[
            pltpu.VMEM((nodes, vec_count, rank), f32),
            pltpu.VMEM((2 * count, vec_count, rank), f32),
            pltpu.VMEM(top_pairs.shape, f32),
            pltpu.VMEM(top_couple.shape, f32),
            pltpu.VMEM(leaf_basis.shape, bf16),
            pltpu.VMEM(near_own.shape, f32),
            pltpu.VMEM(near_got.shape, bf16),
            dma((5,)),
            dma((chunks,)),
        ],
        compiler_params=params,
        name="downward",
    )(
        far_rows,
        far_cols,
        counts,
        ids,
        coefs,
        far_tiles,
        coef_got,
        term_got,
        roots,
        lifts,
        local_transfer,
        top_pairs,
        top_couple,
        leaf_basis,
        near_own,
        near_got,
    )


def solution(mesh):
    in_specs = (
        P(None, "leaf"),
        P(None, "leaf"),
        P("leaf", None, None),
        P("leaf", None, None),
        P("leaf"),
        P("leaf"),
        P("leaf", None, None),
        P("leaf"),
        P("leaf"),
        P("leaf", None),
        P(),
        P(),
    )
    out_specs = P(None, "leaf")
    return jax.shard_map(body, mesh=mesh, in_specs=in_specs, out_specs=out_specs, check_vma=False)
```

```python
import functools

import jax
import jax.numpy as jnp
from jax import lax
from jax.experimental import pallas as pl
from jax.experimental.pallas import tpu as pltpu
from jax.sharding import PartitionSpec as P

f32 = jnp.float32
bf16 = jnp.bfloat16
highest = lax.Precision.HIGHEST
NT = (((1,), (1,)), ((), ()))
VMEM = pl.BlockSpec(memory_space=pltpu.VMEM)
SMEM = pl.BlockSpec(memory_space=pltpu.SMEM)
LIMIT = 56 * 1024 * 1024


def dot(a, b):
    return jnp.dot(a, b, preferred_element_type=f32)


def dot_nt(a, b):
    return lax.dot_general(a, b, NT, preferred_element_type=f32)


def dot_split(a, b):
    high = a.astype(bf16)
    low = (a - high.astype(f32)).astype(bf16)
    rows = a.shape[0]
    both = dot_nt(jnp.concatenate([high, low], axis=0), b)
    return both[:rows] + both[rows:]


def child_pair(transfer_ref, node):
    rank = transfer_ref.shape[1]
    return transfer_ref[node : node + 2].reshape(2 * rank, rank)


def partner_of(me, height):
    mask = 2**height
    return me + mask - 2 * mask * ((me // mask) % 2)


def greet(me, count, reach, heights):
    barrier = pltpu.get_barrier_semaphore()

    def signal(peer):
        pl.semaphore_signal(
            barrier, inc=1, device_id=(peer,), device_id_type=pl.DeviceIdType.MESH
        )

    for step in range(1, reach + 1):

        @pl.when(me - step >= 0)
        def _(step=step):
            signal(me - step)

        @pl.when(me + step < count)
        def _(step=step):
            signal(me + step)

    for height in range(heights):
        signal(partner_of(me, height))
    pl.semaphore_wait(barrier, jnp.minimum(me, reach) + jnp.minimum(count - 1 - me, reach) + heights)


def remote(source, target, send, recv, peer):
    return pltpu.make_async_remote_copy(
        src_ref=source,
        dst_ref=target,
        send_sem=send,
        recv_sem=recv,
        device_id=(peer,),
        device_id_type=pl.DeviceIdType.MESH,
    )


def upward_kernel(
    count,
    leaf_count,
    leaf_size,
    reach,
    vec_ref,
    basis_ref,
    transfer_ref,
    cols_ref,
    coef_ref,
    root_ref,
    ids_ref,
    id_send,
    id_recv,
):
    me = lax.axis_index("leaf")
    nodes = transfer_ref.shape[0]
    greet(me, count, reach, 0)

    def id_copy(step):
        return remote(
            cols_ref, ids_ref.at[step - 1], id_send.at[step - 1], id_recv.at[step - 1], me + step
        )

    for step in range(1, reach + 1):

        @pl.when(me + step < count)
        def _(step=step):
            id_copy(step).start()

    current = []
    for leaf in range(leaf_count):
        span = slice(leaf * leaf_size, (leaf + 1) * leaf_size)
        current.append(dot_nt(vec_ref[:, span], basis_ref[:, span]).astype(bf16))
    offset = 0
    while True:
        for spot, value in enumerate(current):
            coef_ref[offset + spot] = value
        if len(current) == 1:
            break
        parents = []
        for pair in range(len(current) // 2):
            joined = jnp.concatenate([current[2 * pair], current[2 * pair + 1]], axis=1)
            parents.append(dot(joined, child_pair(transfer_ref, offset + 2 * pair)).astype(bf16))
        offset += len(current)
        current = parents
    lift = dot(current[0], transfer_ref[nodes - 1])
    root_ref[...] = jnp.concatenate([current[0].astype(f32), lift], axis=1)

    for step in range(1, reach + 1):

        @pl.when(me + step < count)
        def _(step=step):
            id_copy(step).wait_send()

        @pl.when(me - step >= 0)
        def _(step=step):
            id_copy(step).wait_recv()


def exchange_kernel(
    count,
    cap,
    offsets,
    rows_ref,
    counts_ref,
    ids_ref,
    coef_ref,
    tiles_ref,
    root_ref,
    top_hbm,
    coef_got,
    term_got,
    other_ref,
    coef_buf,
    term_buf,
    top_buf,
    own_buf,
    other_buf,
    coef_send,
    coef_recv,
    term_send,
    term_recv,
    own_send,
    own_recv,
    top_sem,
):
    me = lax.axis_index("leaf")
    reach = offsets - 1
    heights = count.bit_length() - 1
    rank = coef_ref.shape[2]
    lifts = [
        pltpu.make_async_copy(
            top_hbm.at[(count + me) // 2 ** (height + 1) - 2], top_buf.at[height], top_sem.at[height]
        )
        for height in range(heights - 1)
    ]
    for lift in lifts:
        lift.start()
    own_buf[0] = root_ref[...]
    greet(me, count, reach, heights)
    for lift in lifts:
        lift.wait()

    def swap(height):
        return remote(
            own_buf.at[height],
            other_buf.at[height],
            own_send.at[height],
            own_recv.at[height],
            partner_of(me, height),
        )

    def climb(height):
        swap(height).wait()
        other = other_buf[height]
        other_ref[height] = other[:, :rank]
        if height + 1 < heights:
            coef = own_buf[height][:, rank:] + other[:, rank:]
            lift = jnp.dot(coef, top_buf[height], precision=highest, preferred_element_type=f32)
            own_buf[height + 1] = jnp.concatenate([coef, lift], axis=1)
            swap(height + 1).start()

    def back(step):
        at = step - 1
        return remote(coef_buf.at[at], coef_got.at[at], coef_send.at[at], coef_recv.at[at], me - step)

    def ahead(step):
        at = step - 1
        return remote(term_buf.at[at], term_got.at[at], term_send.at[at], term_recv.at[at], me + step)

    swap(0).start()
    height = 0
    for step in range(reach, 0, -1):

        @pl.when(me - step >= 0)
        def _(step=step):
            for pair in range(cap // 2):
                slot = step * cap + 2 * pair
                values = [coef_ref[ids_ref[step - 1, 0, slot + half]] for half in range(2)]
                coef_buf[step - 1, pair] = jnp.concatenate(values, axis=1)
            back(step).start()

        @pl.when(me + step < count)
        def _(step=step):
            for pair in range(cap // 2):
                terms = []
                for half in range(2):
                    spot = 2 * pair + half
                    slot = step * cap + spot
                    term = dot(coef_ref[rows_ref[slot]], tiles_ref[slot])
                    terms.append(jnp.where(spot < counts_ref[step], term, 0.0).astype(bf16))
                term_buf[step - 1, pair] = jnp.concatenate(terms, axis=1)
            ahead(step).start()

        if height < heights:
            climb(height)
            height += 1

    for later in range(height, heights):
        climb(later)

    for step in range(1, reach + 1):

        @pl.when(me - step >= 0)
        def _(step=step):
            back(step).wait_send()
            ahead(step).wait_recv()

        @pl.when(me + step < count)
        def _(step=step):
            ahead(step).wait_send()
            back(step).wait_recv()


def near_kernel(
    group, steps, leaf_size, points, rows_ref, cols_ref, vec_ref, next_ref, tiles_ref, own_ref, spread_ref, joined, total
):
    step = pl.program_id(0)

    @pl.when(step == 0)
    def _():
        joined[:, :points] = vec_ref[...]
        joined[:, points:] = next_ref[...]
        total[...] = jnp.zeros_like(total)

    for spot in range(group):
        tile = tiles_ref[spot]
        row = pl.ds(pl.multiple_of(rows_ref[step * group + spot] * leaf_size, leaf_size), leaf_size)
        col = pl.ds(pl.multiple_of(cols_ref[step * group + spot] * leaf_size, leaf_size), leaf_size)
        to_row = dot_nt(joined[:, col], tile)
        to_col = dot(joined[:, row], tile)
        total[:, row] += to_row
        total[:, col] += to_col

    @pl.when(step == steps - 1)
    def _():
        own_ref[...] = total[:, :points]
        spread_ref[...] = total[:, points:].astype(bf16)


def downward_kernel(
    count,
    cap,
    offsets,
    leaf_count,
    leaf_size,
    chunks,
    rows_ref,
    cols_ref,
    counts_ref,
    ids_ref,
    coef_ref,
    tiles_ref,
    coef_got,
    term_got,
    others_ref,
    transfer_ref,
    top_hbm,
    couple_hbm,
    basis_hbm,
    own_hbm,
    got_hbm,
    out_hbm,
    far,
    top_ref,
    couple_ref,
    basis_ref,
    own_ref,
    got_ref,
    load_sem,
    out_sem,
):
    me = lax.axis_index("leaf")
    rank = coef_ref.shape[1]
    late = [(top_hbm, top_ref), (couple_hbm, couple_ref), (basis_hbm, basis_ref)]
    late += [(own_hbm, own_ref), (got_hbm, got_ref)]
    loads = [pltpu.make_async_copy(a, b, load_sem.at[i]) for i, (a, b) in enumerate(late)]
    for load in loads:
        load.start()
    far[...] = jnp.zeros_like(far)

    to_row = []
    to_col = []
    for spot in range(cap):
        tile = tiles_ref[spot]
        used = spot < counts_ref[0]
        to_row.append(jnp.where(used, dot_nt(coef_ref[cols_ref[spot]], tile), 0.0))
        to_col.append(jnp.where(used, dot(coef_ref[rows_ref[spot]], tile), 0.0))
    for spot in range(cap):
        far[rows_ref[spot]] += to_row[spot]
        far[cols_ref[spot]] += to_col[spot]

    for step in range(1, offsets):

        @pl.when(me + step < count)
        def _(step=step):
            terms = []
            for spot in range(cap):
                half = spot % 2
                values = coef_got[step - 1, spot // 2][:, half * rank : (half + 1) * rank]
                term = dot_nt(values, tiles_ref[step * cap + spot])
                terms.append(jnp.where(spot < counts_ref[step], term, 0.0))
            for spot in range(cap):
                far[rows_ref[step * cap + spot]] += terms[spot]

        @pl.when(me - step >= 0)
        def _(step=step):
            for spot in range(cap):
                half = spot % 2
                values = term_got[step - 1, spot // 2][:, half * rank : (half + 1) * rank]
                far[ids_ref[step - 1, 0, step * cap + spot]] += values.astype(f32)

    loads[0].wait()
    loads[1].wait()
    heights = count.bit_length() - 1
    heap = count + me
    going = None
    for height in range(heights - 1, -1, -1):
        node = heap >> height
        other = others_ref[height]
        tile = couple_ref[(node >> 1) - 1]
        turned = jnp.where(node % 2 == 0, tile.T, tile)
        term = jnp.dot(other, turned, precision=highest, preferred_element_type=f32)
        if going is None:
            going = term
        elif height == 0:
            going = term + dot_split(going, transfer_ref[transfer_ref.shape[0] - 1])
        else:
            lift = top_ref[node - 2]
            going = term + lax.dot_general(going, lift, NT, precision=highest, preferred_element_type=f32)

    offset = far.shape[0] - 1
    current = [far[offset] + going]
    while len(current) < leaf_count:
        offset -= 2 * len(current)
        children = []
        for spot, value in enumerate(current):
            both = dot_split(value, child_pair(transfer_ref, offset + 2 * spot))
            children.append(far[offset + 2 * spot] + both[:, :rank])
            children.append(far[offset + 2 * spot + 1] + both[:, rank:])
        current = children
    for load in loads[2:]:
        load.wait()
    width = leaf_count * leaf_size // chunks
    stores = []
    for leaf, value in enumerate(current):
        span = slice(leaf * leaf_size, (leaf + 1) * leaf_size)
        term = dot(value.astype(bf16), basis_ref[:, span])
        own_ref[:, span] = own_ref[:, span] + got_ref[:, span].astype(f32) + term
        if (leaf + 1) * leaf_size % width == 0:
            part = pl.ds(len(stores) * width, width)
            store = pltpu.make_async_copy(own_ref.at[:, part], out_hbm.at[:, part], out_sem.at[len(stores)])
            store.start()
            stores.append(store)
    for store in stores:
        store.wait()


def body(
    vectors,
    leaf_basis,
    local_transfer,
    near_tiles,
    near_rows,
    near_cols,
    far_tiles,
    far_rows,
    far_cols,
    far_counts,
    top_transfer,
    top_couple,
):
    vec_count, points = vectors.shape
    rank = leaf_basis.shape[0]
    near_count, leaf_size, _ = near_tiles.shape
    leaf_count = points // leaf_size
    nodes = local_transfer.shape[0]
    count = lax.axis_size("leaf")
    slots = far_tiles.shape[0]
    offsets = far_counts.shape[1]
    reach = offsets - 1
    cap = slots // offsets
    counts = far_counts[0]
    params = pltpu.CompilerParams(vmem_limit_bytes=LIMIT)

    following = lax.ppermute(vectors, "leaf", [(source, source - 1) for source in range(1, count)])
    any_space = pl.BlockSpec(memory_space=pl.ANY)
    dma = pltpu.SemaphoreType.DMA
    heights = count.bit_length() - 1

    coefs, root, ids = pl.pallas_call(
        functools.partial(upward_kernel, count, leaf_count, leaf_size, reach),
        out_shape=[
            jax.ShapeDtypeStruct((nodes, vec_count, rank), bf16),
            jax.ShapeDtypeStruct((vec_count, 2 * rank), f32),
            jax.ShapeDtypeStruct((reach, 1, slots), jnp.int32),
        ],
        in_specs=[VMEM] * 3 + [any_space],
        out_specs=[VMEM] * 2 + [any_space],
        scratch_shapes=[dma((reach,))] * 2,
        compiler_params=pltpu.CompilerParams(
            collective_id=0, has_side_effects=True, vmem_limit_bytes=LIMIT
        ),
        name="upward",
    )(vectors, leaf_basis, local_transfer, far_cols.reshape(1, slots))

    group = 8
    steps = near_count // group
    near_own, spread = pl.pallas_call(
        functools.partial(near_kernel, group, steps, leaf_size, points),
        out_shape=[
            jax.ShapeDtypeStruct((vec_count, points), f32),
            jax.ShapeDtypeStruct((vec_count, points), bf16),
        ],
        grid_spec=pltpu.PrefetchScalarGridSpec(
            num_scalar_prefetch=2,
            grid=(steps,),
            in_specs=[
                pl.BlockSpec((vec_count, points), lambda i, *_: (0, 0)),
                pl.BlockSpec((vec_count, points), lambda i, *_: (0, 0)),
                pl.BlockSpec((group, leaf_size, leaf_size), lambda i, *_: (i, 0, 0)),
            ],
            out_specs=[
                pl.BlockSpec((vec_count, points), lambda i, *_: (0, 0)),
                pl.BlockSpec((vec_count, points), lambda i, *_: (0, 0)),
            ],
            scratch_shapes=[
                pltpu.VMEM((vec_count, 2 * points), bf16),
                pltpu.VMEM((vec_count, 2 * points), f32),
            ],
        ),
        compiler_params=params,
        name="near",
    )(near_rows, near_cols, vectors, following, near_tiles)
    spread, coefs = lax.optimization_barrier((spread, coefs))
    near_got = lax.ppermute(spread, "leaf", [(source, source + 1) for source in range(count - 1)])

    packed = (reach, cap // 2, vec_count, 2 * rank)
    coef_got, term_got, others = pl.pallas_call(
        functools.partial(exchange_kernel, count, cap, offsets),
        out_shape=[
            jax.ShapeDtypeStruct(packed, bf16),
            jax.ShapeDtypeStruct(packed, bf16),
            jax.ShapeDtypeStruct((heights, vec_count, rank), f32),
        ],
        in_specs=[SMEM] * 3 + [VMEM] * 3 + [any_space],
        out_specs=[any_space] * 2 + [VMEM],
        scratch_shapes=[pltpu.VMEM(packed, bf16)] * 2
        + [pltpu.VMEM((heights - 1, rank, rank), f32)]
        + [pltpu.VMEM((heights, vec_count, 2 * rank), f32)] * 2
        + [dma((reach,))] * 4
        + [dma((heights,))] * 2
        + [dma((heights - 1,))],
        compiler_params=pltpu.CompilerParams(
            collective_id=1, has_side_effects=True, vmem_limit_bytes=LIMIT
        ),
        name="exchange",
    )(far_rows, counts, ids, coefs, far_tiles, root, top_transfer)

    chunks = 4
    return pl.pallas_call(
        functools.partial(downward_kernel, count, cap, offsets, leaf_count, leaf_size, chunks),
        out_shape=jax.ShapeDtypeStruct((vec_count, points), f32),
        in_specs=[SMEM] * 4 + [VMEM] * 6 + [any_space] * 5,
        out_specs=any_space,
        scratch_shapes=[
            pltpu.VMEM((nodes, vec_count, rank), f32),
            pltpu.VMEM(top_transfer.shape, f32),
            pltpu.VMEM(top_couple.shape, f32),
            pltpu.VMEM(leaf_basis.shape, bf16),
            pltpu.VMEM(near_own.shape, f32),
            pltpu.VMEM(near_got.shape, bf16),
            dma((5,)),
            dma((chunks,)),
        ],
        compiler_params=params,
        name="downward",
    )(
        far_rows,
        far_cols,
        counts,
        ids,
        coefs,
        far_tiles,
        coef_got,
        term_got,
        others,
        local_transfer,
        top_transfer,
        top_couple,
        leaf_basis,
        near_own,
        near_got,
    )


def solution(mesh):
    in_specs = (
        P(None, "leaf"),
        P(None, "leaf"),
        P("leaf", None, None),
        P("leaf", None, None),
        P("leaf"),
        P("leaf"),
        P("leaf", None, None),
        P("leaf"),
        P("leaf"),
        P("leaf", None),
        P(),
        P(),
    )
    out_specs = P(None, "leaf")
    return jax.shard_map(body, mesh=mesh, in_specs=in_specs, out_specs=out_specs, check_vma=False)
```
